512 devices in a mesh: leaf: 32 (over y, x), row: 8 (over z), col: 2 (over core).
Axes of the slice: x: 4, y: 8, z: 8, core: 2. Of those that a mesh axis runs over, the one named last changes fastest.
Arguments:
- leaf_update: float32 [32, 512, 512], P('leaf', 'row', 'col'), as said below
- leaf_rhs: float32 [32, 512, 256], P('leaf', 'row', 'col'), may hold values from -6 to 6
- child_rows: int32 [31, 2, 512], replicated, may hold values from 0 to 1023, as said below
- separator_coef: float32 [31, 512], replicated, may hold values from 0.5 to 4
Outputs:
- final_update: float32 [512, 512], P('row', 'col')
- final_rhs: float32 [512, 256], P('row', 'col')
- separator_solutions: float32 [32, 512, 256], P('leaf', 'row', 'col')
The draws below stay inside these ranges and needn't reach their ends.
Inputs may be any that keep to these rules, and one draw needn't show every extreme that they name: Each child_rows[f, c] lists 512 distinct rows of the front. Each leaf_update[i] is symmetric positive definite.
All inputs are finite; a program needn't handle non-finite values.
Results may differ from the reference program's by a relative error of at most 0.00017.
Values sent between devices are 32-bit elements; how exact they have to be, the bound alone decides.
A program may use at most 128 MiB of HBM per device.

```python
import math
import jax
import jax.numpy as jnp
from jax import lax

K = 512
U = 512
R = 256
F = 1024
FRONTS = 31
N_LEAF = 32


def draw_child_rows(key, part):
    keys_all = jax.random.split(key, FRONTS * 2)
    perms = jax.vmap(lambda one_key: jax.random.permutation(one_key, F))(keys_all)
    return perms[:, :U].reshape(FRONTS, 2, U).astype(jnp.int32)


def draw_leaf_update(key, part):
    key_one = jax.random.fold_in(key, 11)
    factor = jax.random.normal(key_one, (N_LEAF, U, U), jnp.float32)
    product = jnp.einsum('nab,ncb->nac', factor, factor, precision=lax.Precision.HIGHEST) / U
    product = 0.5 * (product + jnp.swapaxes(product, 1, 2))
    positions = jnp.arange(U)
    identity = (positions[:, None] == positions[None, :]).astype(jnp.float32)
    matrix = product + 0.5 * identity[None]
    return matrix.astype(jnp.float32)


def block_levels(rng, shape, cuts, low, high):
    def one(dim, parts):
        steps = jax.random.uniform(jax.random.fold_in(jax.random.fold_in(rng, 6), dim), (parts,), jnp.float32, low / len(cuts), high / len(cuts))
        return jnp.repeat(jnp.exp(steps), shape[dim] // parts).reshape((-1,) + (1,) * (len(shape) - dim - 1))

    factor_of = one(*cuts[0])
    for cut in cuts[1:]:
        factor_of = factor_of * one(*cut)
    return factor_of


def normal_values(key, dims, width, reach, cuts=(), kind=jnp.bfloat16):
    gain = block_levels(key, dims, cuts, -0.22, 0.18) if cuts else 1.0
    entries = jax.random.normal(key, dims, jnp.float32) * width * gain
    return jnp.minimum(jnp.maximum(entries, -reach), reach).astype(kind)


def setup_inputs(seed: int = 0) -> dict:
    key_of = jax.random.split(jax.random.key(seed), 5)
    leaf_update = draw_leaf_update(jax.random.fold_in(key_of[4], 71), 0)
    leaf_rhs = normal_values(key_of[1], (N_LEAF, U, R), 1.0, 6.0, ((0, 32), (1, 8), (2, 2)), jnp.float32)
    child_rows = draw_child_rows(jax.random.fold_in(key_of[4], 71), 0)
    separator_coef = jnp.clip(jnp.exp(jax.random.uniform(key_of[3], (FRONTS, K), jnp.float32, math.log(0.5), math.log(4.0))), 0.5, 4.0)
    return dict(leaf_update=leaf_update, leaf_rhs=leaf_rhs, child_rows=child_rows, separator_coef=separator_coef)


def stencil_block(sep_coefs):
    positions = jnp.arange(sep_coefs.shape[0], dtype=jnp.int32)
    distance = positions[:, None] - positions[None, :]
    return jnp.where(distance == 0, sep_coefs[:, None] + 2.0, jnp.where(jnp.abs(distance) == 1, -1.0, 0.0)).astype(sep_coefs.dtype)

def factor_front(inputs):
    child_upd, child_rhs, row_maps, sep_coefs = inputs
    front_matrix = jnp.zeros((F, F), sep_coefs.dtype)
    front_matrix = front_matrix.at[:K, :K].set(stencil_block(sep_coefs))
    rhs_front = jnp.zeros((F, child_rhs.shape[2]), sep_coefs.dtype)
    for which_child in range(2):
        mapping = row_maps[which_child]
        front_matrix = front_matrix.at[mapping[:, None], mapping[None, :]].add(child_upd[which_child])
        rhs_front = rhs_front.at[mapping].add(child_rhs[which_child])
    lower_factor = jnp.linalg.cholesky(front_matrix[:K, :K])
    panel_rows = jax.scipy.linalg.solve_triangular(lower_factor, front_matrix[K:, :K].T, lower=True)
    schur_block = front_matrix[K:, K:] - jnp.dot(panel_rows.T, panel_rows, precision=lax.Precision.HIGHEST)
    solved = jax.scipy.linalg.solve_triangular(lower_factor, rhs_front[:K], lower=True)
    reduced = rhs_front[K:] - jnp.dot(panel_rows.T, solved, precision=lax.Precision.HIGHEST)
    return (schur_block, reduced, solved)

def reference(leaf_update, leaf_rhs, child_rows, separator_coef):
    levels = N_LEAF.bit_length() - 1
    updates = leaf_update
    reduced = leaf_rhs
    offset = 0
    solved_levels = []
    for level_no in range(1, levels + 1):
        fronts_now = N_LEAF >> level_no
        pairs_upd = updates.reshape(fronts_now, 2, U, U)
        pairs_rhs = reduced.reshape(fronts_now, 2, U, reduced.shape[2])
        updates, reduced, solved = lax.map(factor_front, (pairs_upd, pairs_rhs, child_rows[offset:offset + fronts_now], separator_coef[offset:offset + fronts_now]))
        solved_levels.append(solved)
        offset += fronts_now
    pieces = []
    for device in range(N_LEAF):
        chosen = levels
        for candidate in range(1, levels + 1):
            if device % (1 << candidate) == 1 << candidate - 1:
                chosen = candidate
                break
        pieces.append(solved_levels[chosen - 1][device >> chosen])
    return (updates[0], reduced[0], jnp.stack(pieces))
```

```python
import functools

import jax
import jax.numpy as jnp
from jax import lax
from jax.experimental import pallas as pl
from jax.experimental.pallas import tpu as pltpu
from jax.sharding import PartitionSpec as P

F32 = jnp.float32
BF16 = jnp.bfloat16
MESH = pl.DeviceIdType.MESH
LEVELS = 5
X_LEN, Z_LEN = 4, 8
S = 512
T = 128
FRONT = 2 * S
ROWS = FRONT + T
PAIRS = [(i, j) for i in range(4) for j in range(i + 1)]


def dot_nt(a, b):
    return lax.dot_general(a, b, (((1,), (1,)), ((), ())), preferred_element_type=F32)


def split(x):
    high = x.astype(BF16)
    return high, (x - high.astype(F32)).astype(BF16)


def dot3(ah, al, bh, bl):
    return dot_nt(ah, bh) + dot_nt(ah, bl) + dot_nt(al, bh)


def chol_inverse(a, store_row):
    n = a.shape[0]
    z = (
        lax.broadcasted_iota(jnp.int32, (n, n), 0) == lax.broadcasted_iota(jnp.int32, (n, n), 1)
    ).astype(F32)
    for lo in range(0, n, 8):
        m = n - lo
        cols = [jnp.broadcast_to(a[:, lo + j : lo + j + 1], (m, n)) for j in range(8)]
        top_a, top_z = a[:8], z[:8]
        more = m > 8
        if more:
            a, z = a[8:], z[8:]
        for k in range(8):
            r = lax.rsqrt(cols[k][k : k + 1])
            ck = cols[k] * r
            for j in range(k + 1, 8):
                cols[j] = cols[j] - ck * ck[j : j + 1]
            row_a = top_a[k : k + 1] * r
            row_z = top_z[k : k + 1] * r
            store_row(lo + k, row_z)
            if k < 7:
                top_a = top_a - ck[:8] * row_a
                top_z = top_z - ck[:8] * row_z
            if more:
                a = a - ck[8:] * row_a
                z = z - ck[8:] * row_z


def build_one_hot(map_row, p_ref):
    for lo in range(0, FRONT, 256):
        at = lax.broadcasted_iota(jnp.int32, (256, S), 0) + lo
        p_ref[lo : lo + 256, :] = jnp.where(at == map_row, 1.0, 0.0).astype(BF16)


def spread(item, rhs_t, p_ref, ch, cl, x_ref):
    for p, (i, j) in enumerate(PAIRS):
        block = item[p]
        h, l = split(block)
        ch[i * T : i * T + T, j * T : j * T + T] = h
        cl[i * T : i * T + T, j * T : j * T + T] = l
        if i != j:
            h, l = split(block.T)
            ch[j * T : j * T + T, i * T : i * T + T] = h
            cl[j * T : j * T + T, i * T : i * T + T] = l
    for i in range(4):
        rows = p_ref[i * 256 : i * 256 + 256, :]
        th = dot_nt(rows, ch[...]).astype(BF16)
        tl = dot_nt(rows, cl[...]).astype(BF16)
        for j in range(i + 1):
            cols = p_ref[j * 256 : j * 256 + 256, :]
            x_ref[i * 256 : i * 256 + 256, j * 256 : j * 256 + 256] = dot_nt(th, cols) + dot_nt(
                tl, cols
            )
    hh, hl = split(rhs_t[...])
    for j in range(4):
        cols = p_ref[j * 256 : j * 256 + 256, :]
        x_ref[FRONT:ROWS, j * 256 : j * 256 + 256] = dot_nt(hh, cols) + dot_nt(hl, cols)


def combine(x0, x1, coef_row, a_ref):
    for i in range(4):
        for j in range(i + 1):
            at = (slice(i * 256, i * 256 + 256), slice(j * 256, j * 256 + 256))
            total = x0[at] + x1[at]
            if i < 2:
                distance = (
                    lax.broadcasted_iota(jnp.int32, (256, 256), 0)
                    - lax.broadcasted_iota(jnp.int32, (256, 256), 1)
                    + (i - j) * 256
                )
                diag = coef_row[:, j * 256 : j * 256 + 256] + 2.0
                total = total + jnp.where(
                    distance == 0, diag, jnp.where(jnp.abs(distance) == 1, -1.0, 0.0)
                )
            a_ref[at] = total
    a_ref[FRONT:ROWS, :] = x0[FRONT:ROWS, :] + x1[FRONT:ROWS, :]


def factor(a_ref, li, vh, vl, y_t):
    def block_column(k, _):
        ks = pl.multiple_of(k * T, T)
        here = pl.ds(ks, T)

        def store_row(i, row):
            li[i : i + 1, :] = row

        chol_inverse(a_ref[here, here], store_row)
        lh, ll = split(li[...])
        for lo in range(0, ROWS, 384):
            tile = slice(lo, lo + 384)
            ah, al = split(a_ref[tile, here])
            v = dot3(ah, al, lh, ll)
            h, l = split(v)
            vh[tile, here] = h
            vl[tile, here] = l
            if lo == 768:
                y_t[:, here] = v[256:384]

        def trailing(j, _):
            there = pl.ds(pl.multiple_of(j * T, T), T)
            bh, bl = vh[there, here], vl[there, here]
            for lo in range(0, ROWS, 384):
                tile = slice(lo, lo + 384)
                a_ref[tile, there] = a_ref[tile, there] - dot3(vh[tile, here], vl[tile, here], bh, bl)
            return 0

        lax.fori_loop(k + 1, 4, trailing, 0)
        return 0

    lax.fori_loop(0, 4, block_column, 0)


def schur(a_ref, vh, vl, item, rhs_t):
    for i, j in ((0, 0), (1, 0), (1, 1)):
        ri = slice(S + i * 256, S + i * 256 + 256)
        rj = slice(S + j * 256, S + j * 256 + 256)
        c = a_ref[ri, rj] - dot3(vh[ri, :], vl[ri, :], vh[rj, :], vl[rj, :])
        for p, (bi, bj) in enumerate(PAIRS):
            if bi // 2 == i and bj // 2 == j:
                ro, co = (bi % 2) * T, (bj % 2) * T
                item[p] = c[ro : ro + T, co : co + T]
    rows = slice(FRONT, ROWS)
    for j in range(2):
        rj = slice(S + j * 256, S + j * 256 + 256)
        rhs_t[:, j * 256 : j * 256 + 256] = a_ref[rows, rj] - dot3(
            vh[rows, :], vl[rows, :], vh[rj, :], vl[rj, :]
        )


def partner_of(leaf, t):
    x, y = lax.rem(leaf, X_LEN), leaf // X_LEN
    one = jnp.int32(1)
    span_x = jnp.where(t == 0, 2 * one, jnp.where(t == 1, 4 * one, one))
    span_y = jnp.where(t == 2, 2 * one, jnp.where(t == 3, 4 * one, jnp.where(t == 4, 8 * one, one)))
    px = x - lax.rem(x, span_x) + span_x - 1 - lax.rem(x, span_x)
    py = y - lax.rem(y, span_y) + span_y - 1 - lax.rem(y, span_y)
    return py * X_LEN + px


def kernel(
    upd_ref, rhs_ref, map_ref, coef_ref,
    out_upd, out_rhs, out_sol,
    full, full_h, own, own_h, sib, sib_h, p_own, p_sib, ch, cl, x0, x1, a_ref, li, vh, vl, y_t,
    ring_send, ring_recv, core_send, core_recv,
    put_send, put_recv, fwd_send, fwd_recv, rhs_send, rhs_recv, loc,
):
    leaf = lax.axis_index("leaf")
    row = lax.axis_index("row")
    col = lax.axis_index("col")
    other = 1 - col

    up = lax.rem(row + 1, Z_LEN)
    down = lax.rem(row + Z_LEN - 1, Z_LEN)
    barrier = pltpu.get_barrier_semaphore()
    for target in ((leaf, up, col), (leaf, down, col), (leaf, row, other)):
        pl.semaphore_signal(barrier, inc=1, device_id=target, device_id_type=MESH)
    for t in range(LEVELS):
        target = (partner_of(leaf, t), row, col)
        pl.semaphore_signal(barrier, inc=1, device_id=target, device_id_type=MESH)

    here = (pl.ds(pl.multiple_of(row * 64, 64), 64), pl.ds(pl.multiple_of(col * 256, 256), 256))
    put_u = pltpu.make_async_copy(upd_ref.at[0], full.at[here], loc.at[0])
    put_h = pltpu.make_async_copy(rhs_ref.at[0], full_h.at[here[0]], loc.at[1])
    put_u.start()
    put_h.start()
    put_u.wait()
    put_h.wait()
    pl.semaphore_wait(barrier, 3 + LEVELS)

    def ring_copies(owner, to, way, step):
        rows = pl.ds(pl.multiple_of(owner * 64, 64), 64)
        cols = pl.ds(pl.multiple_of(col * 256, 256), 256)
        made = []
        for n, ref in enumerate((full.at[rows, cols], full_h.at[rows])):
            made.append(
                pltpu.make_async_remote_copy(
                    src_ref=ref, dst_ref=ref,
                    send_sem=ring_send.at[way, step, n], recv_sem=ring_recv.at[way, step, n],
                    device_id=(leaf, to, col), device_id_type=MESH,
                )
            )
        return made

    def core_copy(owner, half, n):
        rows = pl.ds(pl.multiple_of(owner * 64, 64), 64)
        ref = full.at[rows, pl.ds(pl.multiple_of(half * 256, 256), 256)]
        return pltpu.make_async_remote_copy(
            src_ref=ref, dst_ref=ref,
            send_sem=core_send.at[n], recv_sem=core_recv.at[n],
            device_id=(leaf, row, other), device_id_type=MESH,
        )

    sends = []
    owners = [row]
    for copy in ring_copies(row, up, 0, 0) + ring_copies(row, down, 1, 0):
        copy.start()
        sends.append(copy)
    crossing = [core_copy(row, col, 0)]
    crossing[0].start()
    for step in range(4):
        from_down = lax.rem(row + Z_LEN - 1 - step, Z_LEN)
        from_up = lax.rem(row + 1 + step, Z_LEN)
        for way, owner, to in ((0, from_down, up), (1, from_up, down)):
            if way == 1 and step == 3:
                continue
            for copy in ring_copies(owner, to, way, step):
                copy.wait_recv()
            if step + 1 < 4 - way:
                for copy in ring_copies(owner, to, way, step + 1):
                    copy.start()
                    sends.append(copy)
            crossing.append(core_copy(owner, col, len(crossing)))
            crossing[-1].start()
            owners.append(owner)
    for n, owner in enumerate(owners):
        core_copy(owner, other, n).wait_recv()
    for copy in sends + crossing:
        copy.wait_send()

    for p, (i, j) in enumerate(PAIRS):
        own[0, p] = full[i * T : i * T + T, j * T : j * T + T]
    for i in range(4):
        own_h[0, :, i * T : i * T + T] = full_h[i * T : i * T + T, :].T
    out_sol[0] = jnp.zeros((64, T), F32)

    def level(t, _):
        partner = partner_of(leaf, t)
        bit = lax.rem(leaf >> t, 2)
        front = 32 - (32 >> t) + (leaf >> (t + 1))

        def put(q):
            return pltpu.make_async_remote_copy(
                src_ref=own.at[t, 5 * col + q], dst_ref=sib.at[t, 5 * col + q],
                send_sem=put_send.at[q], recv_sem=put_recv.at[t, q],
                device_id=(partner, row, col), device_id_type=MESH,
            )

        def forward(q, half):
            ref = sib.at[t, 5 * half + q]
            return pltpu.make_async_remote_copy(
                src_ref=ref, dst_ref=ref,
                send_sem=fwd_send.at[q], recv_sem=fwd_recv.at[t, q],
                device_id=(leaf, row, other), device_id_type=MESH,
            )

        put_rhs = pltpu.make_async_remote_copy(
            src_ref=own_h.at[t], dst_ref=sib_h.at[t],
            send_sem=rhs_send, recv_sem=rhs_recv.at[t],
            device_id=(partner, row, col), device_id_type=MESH,
        )
        for q in range(5):
            put(q).start()
        put_rhs.start()
        build_one_hot(map_ref[pl.ds(2 * front + bit, 1), :], p_own)
        build_one_hot(map_ref[pl.ds(2 * front + 1 - bit, 1), :], p_sib)
        spread(own.at[t], own_h.at[t], p_own, ch, cl, x0)
        for q in range(5):
            put(q).wait_recv()
            forward(q, col).start()
        for q in range(5):
            forward(q, other).wait_recv()
        put_rhs.wait_recv()
        spread(sib.at[t], sib_h.at[t], p_sib, ch, cl, x1)
        for q in range(5):
            put(q).wait_send()
            forward(q, col).wait_send()
        put_rhs.wait_send()
        combine(x0, x1, coef_ref[pl.ds(front, 1), :], a_ref)
        factor(a_ref, li, vh, vl, y_t)
        schur(a_ref, vh, vl, own.at[t + 1], own_h.at[t + 1])

        low = lax.rem(leaf, 2 << t)
        keep = (low == (1 << t)) | ((t == LEVELS - 1) & (lax.rem(leaf, 1 << t) == 0))

        @pl.when(keep)
        def _():
            block = y_t[:, pl.ds(pl.multiple_of(row // 2 * T, T), T)].T
            li[...] = block
            out_sol[0] = li[pl.ds(pl.multiple_of(lax.rem(row, 2) * 64, 64), 64), :]

        return 0

    lax.fori_loop(0, LEVELS, level, 0)

    for p, (i, j) in enumerate(PAIRS):
        block = own[LEVELS, p]
        full[i * T : i * T + T, j * T : j * T + T] = block
        if i != j:
            full[j * T : j * T + T, i * T : i * T + T] = block.T
    for i in range(4):
        full_h[i * T : i * T + T, :] = own_h[LEVELS, :, i * T : i * T + T].T
    out_upd[...] = full[here]
    out_rhs[...] = full_h[here[0], :]


def per_device(leaf_update, leaf_rhs, child_rows, separator_coef):
    vmem = pl.BlockSpec(memory_space=pltpu.VMEM)
    dma = pltpu.SemaphoreType.DMA
    return pl.pallas_call(
        kernel,
        name="multifrontal",
        out_shape=(
            jax.ShapeDtypeStruct((64, 256), F32),
            jax.ShapeDtypeStruct((64, T), F32),
            jax.ShapeDtypeStruct((1, 64, T), F32),
        ),
        in_specs=[vmem] * 4,
        out_specs=(vmem,) * 3,
        scratch_shapes=[
            pltpu.VMEM((S, S), F32),
            pltpu.VMEM((S, T), F32),
            pltpu.VMEM((LEVELS + 1, 10, T, T), F32),
            pltpu.VMEM((LEVELS + 1, T, S), F32),
            pltpu.VMEM((LEVELS, 10, T, T), F32),
            pltpu.VMEM((LEVELS, T, S), F32),
            pltpu.VMEM((FRONT, S), BF16),
            pltpu.VMEM((FRONT, S), BF16),
            pltpu.VMEM((S, S), BF16),
            pltpu.VMEM((S, S), BF16),
            pltpu.VMEM((ROWS, FRONT), F32),
            pltpu.VMEM((ROWS, FRONT), F32),
            pltpu.VMEM((ROWS, FRONT), F32),
            pltpu.VMEM((T, T), F32),
            pltpu.VMEM((ROWS, S), BF16),
            pltpu.VMEM((ROWS, S), BF16),
            pltpu.VMEM((T, S), F32),
            dma((2, 4, 2)),
            dma((2, 4, 2)),
            dma((8,)),
            dma((8,)),
            dma((5,)),
            dma((LEVELS, 5)),
            dma((5,)),
            dma((LEVELS, 5)),
            dma,
            dma((LEVELS,)),
            dma((2,)),
        ],
        compiler_params=pltpu.CompilerParams(
            collective_id=0, has_side_effects=True, vmem_limit_bytes=56 * 1024 * 1024
        ),
    )(leaf_update, leaf_rhs, child_rows.reshape(-1, S), separator_coef)


def solution(mesh):
    in_specs = (P("leaf", "row", "col"), P("leaf", "row", "col"), P(), P())
    out_specs = (P("row", "col"), P("row", "col"), P("leaf", "row", "col"))
    return jax.shard_map(
        per_device, mesh=mesh, in_specs=in_specs, out_specs=out_specs, check_vma=False
    )
```

```python
import functools

import jax
import jax.numpy as jnp
from jax import lax
from jax.experimental import pallas as pl
from jax.experimental.pallas import tpu as pltpu
from jax.sharding import PartitionSpec as P

F32 = jnp.float32
BF16 = jnp.bfloat16
MESH = pl.DeviceIdType.MESH
LEVELS = 5
X_LEN, Z_LEN = 4, 8
S = 512
T = 128
FRONT = 2 * S
ROWS = FRONT + 16
PAIRS = [(i, j) for i in range(4) for j in range(i + 1)]


def dot_nt(a, b):
    return lax.dot_general(a, b, (((1,), (1,)), ((), ())), preferred_element_type=F32)


def split(x):
    high = x.astype(BF16)
    return high, (x - high.astype(F32)).astype(BF16)


def dot_tn(a, b):
    return lax.dot_general(a, b, (((0,), (0,)), ((), ())), preferred_element_type=F32)


def dot3(ah, al, bh, bl):
    return dot_nt(ah, bh) + dot_nt(ah, bl) + dot_nt(al, bh)


def eliminate(a, base, store_row):
    m, n = a.shape
    lane = lax.broadcasted_iota(jnp.int32, (8, n), 1)
    sub = lax.broadcasted_iota(jnp.int32, (8, n), 0)

    def spread_col(rows, at):
        return jnp.broadcast_to(rows[:, at : at + 1], rows.shape)

    top = [spread_col(a[:8], base + j) for j in range(8)]
    for lo in range(0, m, 8):
        at = base + lo
        inside = (lane >= at) & (lane < at + 8)
        head = jnp.where(inside, jnp.where(lane - at == sub, 1.0, 0.0), a[:8])
        left = m - lo - 8
        if left:
            low = [spread_col(a[8:], at + j) for j in range(8)]
            ahead = [spread_col(a[8:16], at + 8 + j) for j in range(8)]
            a = jnp.concatenate(
                [jnp.where(inside, 0.0, a[i : i + 8]) for i in range(8, left + 8, 8)], axis=0
            )
        for k in range(8):
            pivot = top[k][k : k + 1]
            inverse = 1.0 / pivot
            row = head[k : k + 1]
            store_row(lo + k, row * lax.rsqrt(pivot))
            if left:
                below = low[k] * inverse
            for j in range(k + 1, 8):
                factor_row = top[k][j : j + 1]
                top[j] = top[j] - (top[k] * factor_row) * inverse
                if left:
                    low[j] = low[j] - below * factor_row
            if left:
                for j in range(8):
                    ahead[j] = ahead[j] - below[:8] * low[k][j : j + 1]
                a = a - below * row
            if k < 7:
                head = head - (top[k] * inverse) * row
        if left:
            top = ahead


def build_one_hot(map_row, p_ref):
    for lo in range(0, FRONT, 256):
        at = lax.broadcasted_iota(jnp.int32, (256, S), 0) + lo
        p_ref[lo : lo + 256, :] = jnp.where(at == map_row, 1.0, 0.0).astype(BF16)


def expand(item, ch, cl):
    for p, (i, j) in enumerate(PAIRS):
        block = jnp.concatenate([item[2 * p], item[2 * p + 1]], axis=0)
        h, l = split(block)
        ch[i * T : i * T + T, j * T : j * T + T] = h
        cl[i * T : i * T + T, j * T : j * T + T] = l
        if i != j:
            h, l = split(block.T)
            ch[j * T : j * T + T, i * T : i * T + T] = h
            cl[j * T : j * T + T, i * T : i * T + T] = l


def spread_rows(i, p_ref, ch, cl, th, tl):
    tile = slice(i * 256, i * 256 + 256)
    rows = p_ref[tile, :]
    th[tile, :] = dot_nt(rows, ch[...]).astype(BF16)
    tl[tile, :] = dot_nt(rows, cl[...]).astype(BF16)


def spread_cols(i, p_ref, th, tl, x_ref):
    tile = slice(i * 256, i * 256 + 256)
    for j in range(i + 1):
        cols = p_ref[j * 256 : j * 256 + 256, :]
        x_ref[tile, j * 256 : j * 256 + 256] = dot_nt(th[tile, :], cols) + dot_nt(tl[tile, :], cols)


def spread_rhs(rhs_t, p_ref, x_ref):
    both = jnp.concatenate(split(rhs_t[...]), axis=0)
    for j in range(4):
        x = dot_nt(both, p_ref[j * 256 : j * 256 + 256, :])
        x_ref[FRONT:ROWS, j * 256 : j * 256 + 256] = x[:16] + x[16:]


def combine(x0, x1, coef_row, a_ref):
    for i in range(4):
        for j in range(i + 1):
            at = (slice(i * 256, i * 256 + 256), slice(j * 256, j * 256 + 256))
            total = x0[at] + x1[at]
            if i < 2:
                distance = (
                    lax.broadcasted_iota(jnp.int32, (256, 256), 0)
                    - lax.broadcasted_iota(jnp.int32, (256, 256), 1)
                    + (i - j) * 256
                )
                diag = coef_row[:, j * 256 : j * 256 + 256] + 2.0
                total = total + jnp.where(
                    distance == 0, diag, jnp.where(jnp.abs(distance) == 1, -1.0, 0.0)
                )
            a_ref[at] = total
    a_ref[FRONT:ROWS, :] = x0[FRONT:ROWS, :] + x1[FRONT:ROWS, :]


def factor(a_ref, li, raw, diag, vh, vl, y_t):
    vh[...] = jnp.zeros_like(vh)
    vl[...] = jnp.zeros_like(vl)
    li[...] = jnp.zeros_like(li)
    diag[...] = a_ref[0:T, 0:T]
    tiles = [slice(0, 256), slice(256, 512), slice(512, 768), slice(768, ROWS)]

    def panel(k):
        here = pl.ds(pl.multiple_of(k * T, T), T)
        lh, ll = split(li[...])
        for tile in tiles:
            ah, al = split(a_ref[tile, here])
            v = dot3(ah, al, lh, ll)
            h, l = split(v)
            vh[tile, here] = h
            vl[tile, here] = l
            if tile.stop == ROWS:
                y_t[:, here] = v[256:]

    def block_column(k, _):
        here = pl.ds(pl.multiple_of(k * T, T), T)
        after = pl.ds(pl.multiple_of(k * T + T, T), T)
        block = diag[...]

        def store_upper(i, row):
            raw[i : i + 1, :] = row

        def store_lower(i, row):
            raw[64 + i : 65 + i, :] = row

        eliminate(block[:64], 0, store_upper)
        panel(jnp.maximum(k - 1, 0))
        lanes = lax.broadcasted_iota(jnp.int32, (64, T), 1)
        valid = (lanes <= lax.broadcasted_iota(jnp.int32, (64, T), 0)) | (lanes >= 64)
        rh, rl = split(jnp.where(valid, raw[0:64, :], 0.0))
        lower = jnp.where(lanes < 64, 0.0, block[64:])
        lower = lower - (dot_tn(rh, rh) + dot_tn(rh, rl) + dot_tn(rl, rh))[64:]
        eliminate(lower, 64, store_lower)
        bh, bl = vh[here, :], vl[here, :]
        for tile in tiles:
            a_ref[tile, here] = a_ref[tile, here] - dot3(vh[tile, :], vl[tile, :], bh, bl)
        nh, nl = vh[after, :], vl[after, :]
        next_block = a_ref[after, after] - dot3(nh, nl, nh, nl)
        at = lax.broadcasted_iota(jnp.int32, (T, T), 0)
        inverse = jnp.where(lax.broadcasted_iota(jnp.int32, (T, T), 1) <= at, raw[...], 0.0)
        li[...] = inverse
        lh, ll = split(inverse)
        ah, al = split(a_ref[after, here])
        h, l = split(dot3(ah, al, lh, ll))
        diag[...] = next_block - dot3(h, l, h, l)
        vh[after, here] = h
        vl[after, here] = l
        return 0

    lax.fori_loop(0, 4, block_column, 0)
    panel(3)


def schur(a_ref, vh, vl, item):
    for i, j in ((0, 0), (1, 0), (1, 1)):
        ri = slice(S + i * 256, S + i * 256 + 256)
        rj = slice(S + j * 256, S + j * 256 + 256)
        c = a_ref[ri, rj] - dot3(vh[ri, :], vl[ri, :], vh[rj, :], vl[rj, :])
        for p, (bi, bj) in enumerate(PAIRS):
            if bi // 2 == i and bj // 2 == j:
                ro, co = (bi % 2) * T, (bj % 2) * T
                item[2 * p] = c[ro : ro + 64, co : co + T]
                item[2 * p + 1] = c[ro + 64 : ro + T, co : co + T]


def schur_rhs(a_ref, vh, vl, rhs_t):
    rows = slice(FRONT, ROWS)
    for j in range(2):
        rj = slice(S + j * 256, S + j * 256 + 256)
        rhs_t[:, j * 256 : j * 256 + 256] = a_ref[rows, rj] - dot3(
            vh[rows, :], vl[rows, :], vh[rj, :], vl[rj, :]
        )


def partner_of(leaf, t):
    x, y = lax.rem(leaf, X_LEN), leaf // X_LEN
    one = jnp.int32(1)
    span_x = jnp.where(t == 0, 2 * one, jnp.where(t == 1, 4 * one, one))
    span_y = jnp.where(t == 2, 2 * one, jnp.where(t == 3, 4 * one, jnp.where(t == 4, 8 * one, one)))
    px = x - lax.rem(x, span_x) + span_x - 1 - lax.rem(x, span_x)
    py = y - lax.rem(y, span_y) + span_y - 1 - lax.rem(y, span_y)
    return py * X_LEN + px


def kernel(
    upd_ref, rhs_ref, map_ref, coef_ref,
    out_upd, out_rhs, out_sol,
    full, slab_out, slab_in, last_out, last_in,
    own, own_h, sib, sib_h, p_own, p_sib, ch, cl, th, tl, x0, x1, a_ref, li, raw, diag, vh, vl, y_t, y_kept,
    ring_send, ring_recv, core_send, core_recv, slab_send, slab_recv, last_send, last_recv,
    put_send, put_recv, row_send, row_recv, near_send, near_recv, far_send, far_recv,
    rhs_send, rhs_recv, loc,
):
    leaf = lax.axis_index("leaf")
    row = lax.axis_index("row")
    col = lax.axis_index("col")
    other = 1 - col
    beside = row + 1 - 2 * lax.rem(row, 2)
    quarter = 2 * lax.rem(row, 2) + col
    quarter_row = 2 * lax.rem(beside, 2) + col

    def to_peer(src, dst, send_sem, recv_sem, device):
        return pltpu.make_async_remote_copy(
            src_ref=src, dst_ref=dst, send_sem=send_sem, recv_sem=recv_sem,
            device_id=device, device_id_type=MESH,
        )

    barrier = pltpu.get_barrier_semaphore()
    peers = [lax.rem(row + d, Z_LEN) for d in range(Z_LEN)]
    targets = [(leaf, peers[d], col) for d in range(1, Z_LEN)] + [(leaf, row, other)]
    targets += [(partner_of(leaf, t), row, col) for t in range(LEVELS)]
    for target in targets:
        pl.semaphore_signal(barrier, inc=1, device_id=target, device_id_type=MESH)

    here = (pl.ds(pl.multiple_of(row * 64, 64), 64), pl.ds(pl.multiple_of(col * 256, 256), 256))
    put_own = pltpu.make_async_copy(upd_ref.at[0], full.at[here], loc)
    put_own.start()
    slabs = rhs_ref[0].T
    for r in range(Z_LEN):
        slab_out[r, :, 0:64] = slabs[r * 16 : r * 16 + 16, :]
    put_own.wait()
    pl.semaphore_wait(barrier, len(targets))

    up, down = peers[1], peers[Z_LEN - 1]

    def ring_copy(owner, to, way, step):
        rows = pl.ds(pl.multiple_of(owner * 64, 64), 64)
        ref = full.at[rows, here[1]]
        return to_peer(
            ref, ref, ring_send.at[way, step], ring_recv.at[way, step], (leaf, to, col)
        )

    def core_copy(owner, half, n):
        rows = pl.ds(pl.multiple_of(owner * 64, 64), 64)
        ref = full.at[rows, pl.ds(pl.multiple_of(half * 256, 256), 256)]
        return to_peer(ref, ref, core_send.at[n], core_recv.at[n], (leaf, row, other))

    sends = [ring_copy(row, up, 0, 0), ring_copy(row, down, 1, 0), core_copy(row, col, 0)]
    for copy in sends:
        copy.start()
    slab_copies = [
        to_peer(
            slab_out.at[peers[d]], slab_in.at[row], slab_send.at[d], slab_recv.at[d],
            (leaf, peers[d], col),
        )
        for d in range(1, Z_LEN)
    ]
    for copy in slab_copies:
        copy.start()
    slab_in[row] = slab_out[row]
    owners = [row]
    for step in range(4):
        for way, owner, to in ((0, peers[7 - step], up), (1, peers[1 + step], down)):
            if way == 1 and step == 3:
                continue
            ring_copy(owner, to, way, step).wait_recv()
            if step + 1 < 4 - way:
                sends.append(ring_copy(owner, to, way, step + 1))
                sends[-1].start()
            sends.append(core_copy(owner, col, len(owners)))
            sends[-1].start()
            owners.append(owner)
    for n, owner in enumerate(owners):
        core_copy(owner, other, n).wait_recv()
    for copy in sends:
        copy.wait_send()
    for copy in slab_copies:
        copy.wait()

    def puts(t):
        partner = partner_of(leaf, t)
        return [
            to_peer(
                own.at[t, 5 * quarter + q], sib.at[t, 5 * quarter + q],
                put_send.at[q], put_recv.at[t, q], (partner, row, col),
            )
            for q in range(5)
        ]

    def put_rhs(t):
        return to_peer(
            own_h.at[t], sib_h.at[t], rhs_send, rhs_recv.at[t], (partner_of(leaf, t), row, col)
        )

    for p, (i, j) in enumerate(PAIRS):
        for half in range(2):
            lo = i * T + half * 64
            own[0, 2 * p + half] = full[lo : lo + 64, j * T : j * T + T]
    for copy in puts(0):
        copy.start()
    for i in range(4):
        own_h[0, :, i * T : i * T + T] = jnp.concatenate(
            [slab_in[2 * i, :, 0:64], slab_in[2 * i + 1, :, 0:64]], axis=1
        )
    put_rhs(0).start()

    def level(t, _):
        bit = lax.rem(leaf >> t, 2)
        front = 32 - (32 >> t) + (leaf >> (t + 1))

        def share(part, q, send, recv, device):
            ref = sib.at[t, 5 * part + q]
            return to_peer(ref, ref, send.at[q], recv.at[t, q], device)

        over_core, over_row = (leaf, row, other), (leaf, beside, col)
        arrive = puts(t)
        to_near = [share(quarter, q, near_send, near_recv, over_core) for q in range(5)]
        to_row = [share(quarter, q, row_send, row_recv, over_row) for q in range(5)]
        to_far = [share(quarter_row, q, far_send, far_recv, over_core) for q in range(5)]

        def pass_on(q):
            arrive[q].wait_recv()
            to_row[q].start()
            to_near[q].start()

        def pass_far(q):
            to_row[q].wait_recv()
            to_far[q].start()

        build_one_hot(map_ref[front, pl.ds(bit, 1), :], p_own)
        expand(own.at[t], ch, cl)
        spread_rows(0, p_own, ch, cl, th, tl)
        spread_cols(0, p_own, th, tl, x0)
        pass_on(0)
        spread_rows(1, p_own, ch, cl, th, tl)
        pass_on(1)
        spread_cols(1, p_own, th, tl, x0)
        pass_on(2)
        spread_rows(2, p_own, ch, cl, th, tl)
        pass_on(3)
        pass_far(0)
        spread_cols(2, p_own, th, tl, x0)
        pass_on(4)
        pass_far(1)
        spread_rows(3, p_own, ch, cl, th, tl)
        pass_far(2)
        spread_cols(3, p_own, th, tl, x0)
        pass_far(3)
        build_one_hot(map_ref[front, pl.ds(1 - bit, 1), :], p_sib)
        pass_far(4)
        spread_rhs(own_h.at[t], p_own, x0)
        put_rhs(t).wait()
        spread_rhs(sib_h.at[t], p_sib, x1)
        for q in range(5):
            to_near[q].wait_recv()
            to_far[q].wait_recv()
        expand(sib.at[t], ch, cl)
        for i in range(4):
            spread_rows(i, p_sib, ch, cl, th, tl)
            spread_cols(i, p_sib, th, tl, x1)
        for q in range(5):
            for copy in (arrive[q], to_near[q], to_row[q], to_far[q]):
                copy.wait_send()
        combine(x0, x1, coef_ref[pl.ds(front, 1), :], a_ref)
        factor(a_ref, li, raw, diag, vh, vl, y_t)
        schur(a_ref, vh, vl, own.at[t + 1])

        @pl.when(t < LEVELS - 1)
        def _():
            for copy in puts(t + 1):
                copy.start()

        schur_rhs(a_ref, vh, vl, own_h.at[t + 1])

        @pl.when(t < LEVELS - 1)
        def _():
            put_rhs(t + 1).start()

        low = lax.rem(leaf, 2 << t)
        keep = (low == (1 << t)) | ((t == LEVELS - 1) & (lax.rem(leaf, 1 << t) == 0))

        @pl.when(keep)
        def _():
            y_kept[...] = y_t[...]

        return 0

    lax.fori_loop(0, LEVELS, level, 0)

    for r in range(Z_LEN):
        last_out[r, 0:16, 0:64] = own_h[LEVELS, :, r * 64 : r * 64 + 64]
        last_out[r, 16:32, 0:64] = y_kept[:, r * 64 : r * 64 + 64]
    last_copies = [
        to_peer(
            last_out.at[peers[d]], last_in.at[row], last_send.at[d], last_recv.at[d],
            (leaf, peers[d], col),
        )
        for d in range(1, Z_LEN)
    ]
    for copy in last_copies:
        copy.start()
    last_in[row] = last_out[row]
    for p, (i, j) in enumerate(PAIRS):
        block = jnp.concatenate([own[LEVELS, 2 * p], own[LEVELS, 2 * p + 1]], axis=0)
        full[i * T : i * T + T, j * T : j * T + T] = block
        if i != j:
            full[j * T : j * T + T, i * T : i * T + T] = block.T
    out_upd[...] = full[here]
    for copy in last_copies:
        copy.wait()
    out_rhs[...] = jnp.concatenate([last_in[r, 0:16, 0:64] for r in range(Z_LEN)], axis=0).T
    out_sol[0] = jnp.concatenate([last_in[r, 16:32, 0:64] for r in range(Z_LEN)], axis=0).T


def per_device(leaf_update, leaf_rhs, child_rows, separator_coef):
    vmem = pl.BlockSpec(memory_space=pltpu.VMEM)
    dma = pltpu.SemaphoreType.DMA
    return pl.pallas_call(
        kernel,
        name="multifrontal",
        out_shape=(
            jax.ShapeDtypeStruct((64, 256), F32),
            jax.ShapeDtypeStruct((64, T), F32),
            jax.ShapeDtypeStruct((1, 64, T), F32),
        ),
        in_specs=[vmem] * 4,
        out_specs=(vmem,) * 3,
        scratch_shapes=[
            pltpu.VMEM((S, S), F32),
            pltpu.VMEM((Z_LEN, 16, T), F32),
            pltpu.VMEM((Z_LEN, 16, T), F32),
            pltpu.VMEM((Z_LEN, 32, T), F32),
            pltpu.VMEM((Z_LEN, 32, T), F32),
            pltpu.VMEM((LEVELS + 1, 20, 64, T), F32),
            pltpu.VMEM((LEVELS + 1, 16, S), F32),
            pltpu.VMEM((LEVELS, 20, 64, T), F32),
            pltpu.VMEM((LEVELS, 16, S), F32),
            pltpu.VMEM((FRONT, S), BF16),
            pltpu.VMEM((FRONT, S), BF16),
            pltpu.VMEM((S, S), BF16),
            pltpu.VMEM((S, S), BF16),
            pltpu.VMEM((FRONT, S), BF16),
            pltpu.VMEM((FRONT, S), BF16),
            pltpu.VMEM((ROWS, FRONT), F32),
            pltpu.VMEM((ROWS, FRONT), F32),
            pltpu.VMEM((ROWS, FRONT), F32),
            pltpu.VMEM((T, T), F32),
            pltpu.VMEM((T, T), F32),
            pltpu.VMEM((T, T), F32),
            pltpu.VMEM((ROWS, S), BF16),
            pltpu.VMEM((ROWS, S), BF16),
            pltpu.VMEM((16, S), F32),
            pltpu.VMEM((16, S), F32),
            dma((2, 4)), dma((2, 4)),
            dma((8,)), dma((8,)),
            dma((8,)), dma((8,)),
            dma((8,)), dma((8,)),
            dma((5,)), dma((LEVELS, 5)),
            dma((5,)), dma((LEVELS, 5)),
            dma((5,)), dma((LEVELS, 5)),
            dma((5,)), dma((LEVELS, 5)),
            dma, dma((LEVELS,)),
            dma,
        ],
        compiler_params=pltpu.CompilerParams(
            collective_id=0, has_side_effects=True, vmem_limit_bytes=56 * 1024 * 1024
        ),
    )(leaf_update, leaf_rhs, child_rows, separator_coef)


def solution(mesh):
    in_specs = (P("leaf", "row", "col"), P("leaf", "row", "col"), P(), P())
    out_specs = (P("row", "col"), P("row", "col"), P("leaf", "row", "col"))
    return jax.shard_map(
        per_device, mesh=mesh, in_specs=in_specs, out_specs=out_specs, check_vma=False
    )
```

```python
import functools

import jax
import jax.numpy as jnp
from jax import lax
from jax.experimental import pallas as pl
from jax.experimental.pallas import tpu as pltpu
from jax.sharding import PartitionSpec as P

F32 = jnp.float32
BF16 = jnp.bfloat16
MESH = pl.DeviceIdType.MESH
LEVELS = 5
X_LEN, Z_LEN = 4, 8
S = 512
T = 128
FRONT = 2 * S
ROWS = FRONT + 16
PAIRS = [(i, j) for i in range(4) for j in range(i + 1)]


def dot_nt(a, b):
    return lax.dot_general(a, b, (((1,), (1,)), ((), ())), preferred_element_type=F32)


def split(x):
    high = x.astype(BF16)
    return high, (x - high.astype(F32)).astype(BF16)


def dot_tn(a, b):
    return lax.dot_general(a, b, (((0,), (0,)), ((), ())), preferred_element_type=F32)


def dot3(ah, al, bh, bl):
    return dot_nt(ah, bh) + dot_nt(ah, bl) + dot_nt(al, bh)


def eliminate(a, base, store_row):
    m, n = a.shape
    lane = lax.broadcasted_iota(jnp.int32, (8, n), 1)
    sub = lax.broadcasted_iota(jnp.int32, (8, n), 0)

    def spread_col(rows, at):
        return jnp.broadcast_to(rows[:, at : at + 1], rows.shape)

    top = [spread_col(a[:8], base + j) for j in range(8)]
    for lo in range(0, m, 8):
        at = base + lo
        inside = (lane >= at) & (lane < at + 8)
        head = jnp.where(inside, jnp.where(lane - at == sub, 1.0, 0.0), a[:8])
        left = m - lo - 8
        if left:
            low = [spread_col(a[8:], at + j) for j in range(8)]
            ahead = [spread_col(a[8:16], at + 8 + j) for j in range(8)]
            a = jnp.concatenate(
                [jnp.where(inside, 0.0, a[i : i + 8]) for i in range(8, left + 8, 8)], axis=0
            )
        for k in range(8):
            pivot = top[k][k : k + 1]
            inverse = 1.0 / pivot
            row = head[k : k + 1]
            store_row(lo + k, row * lax.rsqrt(pivot))
            if left:
                below = low[k] * inverse
            for j in range(k + 1, 8):
                factor_row = top[k][j : j + 1]
                top[j] = top[j] - (top[k] * factor_row) * inverse
                if left:
                    low[j] = low[j] - below * factor_row
            if left:
                for j in range(8):
                    ahead[j] = ahead[j] - below[:8] * low[k][j : j + 1]
                a = a - below * row
            if k < 7:
                head = head - (top[k] * inverse) * row
        if left:
            top = ahead


def build_one_hot(map_row, p_ref):
    for lo in range(0, FRONT, 256):
        at = lax.broadcasted_iota(jnp.int32, (256, S), 0) + lo
        p_ref[lo : lo + 256, :] = jnp.where(at == map_row, 1.0, 0.0).astype(BF16)


def expand(item, ch, cl):
    for p, (i, j) in enumerate(PAIRS):
        block = jnp.concatenate([item[2 * p], item[2 * p + 1]], axis=0)
        h, l = split(block)
        ch[i * T : i * T + T, j * T : j * T + T] = h
        cl[i * T : i * T + T, j * T : j * T + T] = l
        if i != j:
            h, l = split(block.T)
            ch[j * T : j * T + T, i * T : i * T + T] = h
            cl[j * T : j * T + T, i * T : i * T + T] = l


def spread_rows(i, p_ref, ch, cl, th, tl):
    tile = slice(i * 256, i * 256 + 256)
    rows = p_ref[tile, :]
    th[tile, :] = dot_nt(rows, ch[...]).astype(BF16)
    tl[tile, :] = dot_nt(rows, cl[...]).astype(BF16)


def spread_cols(i, p_ref, th, tl, x_ref, first=0):
    tile = slice(i * 256, i * 256 + 256)
    for j in range(first, i + 1):
        cols = p_ref[j * 256 : j * 256 + 256, :]
        x_ref[tile, j * 256 : j * 256 + 256] = dot_nt(th[tile, :], cols) + dot_nt(tl[tile, :], cols)


def spread_rhs(rhs_t, p_ref, x_ref):
    both = jnp.concatenate(split(rhs_t[...]), axis=0)
    for j in range(4):
        x = dot_nt(both, p_ref[j * 256 : j * 256 + 256, :])
        x_ref[FRONT:ROWS, j * 256 : j * 256 + 256] = x[:16] + x[16:]


def combine(x0, x1, coef_row, a_ref):
    for i, j in ((0, 0), (1, 0), (1, 1)):
        at = (slice(i * 256, i * 256 + 256), slice(j * 256, j * 256 + 256))
        distance = (
            lax.broadcasted_iota(jnp.int32, (256, 256), 0)
            - lax.broadcasted_iota(jnp.int32, (256, 256), 1)
            + (i - j) * 256
        )
        diag = coef_row[:, j * 256 : j * 256 + 256] + 2.0
        stencil = jnp.where(distance == 0, diag, jnp.where(jnp.abs(distance) == 1, -1.0, 0.0))
        a_ref[at] = x0[at] + x1[at] + stencil
    for i, j in ((2, 2), (3, 2), (3, 3)):
        at = (slice(i * 256, i * 256 + 256), slice(j * 256, j * 256 + 256))
        a_ref[at] = x0[at] + x1[at]
    a_ref[FRONT:ROWS, :] = x0[FRONT:ROWS, :] + x1[FRONT:ROWS, :]


def clear(li, vh, vl):
    vh[...] = jnp.zeros_like(vh)
    vl[...] = jnp.zeros_like(vl)
    li[...] = jnp.zeros_like(li)


def factor(a_ref, x0, x1, p_sib, th, tl, li, raw, diag, vh, vl, y_t):
    diag[...] = a_ref[0:T, 0:T]
    tiles = [slice(0, 256), slice(256, 512), slice(512, 768), slice(768, ROWS)]

    def panel(k):
        here = pl.ds(pl.multiple_of(k * T, T), T)
        lh, ll = split(li[...])
        for tile in tiles:
            ah, al = split(a_ref[tile, here])
            v = dot3(ah, al, lh, ll)
            h, l = split(v)
            vh[tile, here] = h
            vl[tile, here] = l
            if tile.stop == ROWS:
                y_t[:, here] = v[256:]

    def block_column(k, _):
        here = pl.ds(pl.multiple_of(k * T, T), T)
        after = pl.ds(pl.multiple_of(k * T + T, T), T)
        block = diag[...]

        def store_upper(i, row):
            raw[i : i + 1, :] = row

        def store_lower(i, row):
            raw[64 + i : 65 + i, :] = row

        eliminate(block[:64], 0, store_upper)
        panel(jnp.maximum(k - 1, 0))
        for tile in (slice(512, 768), slice(768, FRONT)):
            x1[tile, here] = dot_nt(th[tile, :], p_sib[here, :]) + dot_nt(tl[tile, :], p_sib[here, :])
            a_ref[tile, here] = x0[tile, here] + x1[tile, here]
        lanes = lax.broadcasted_iota(jnp.int32, (64, T), 1)
        valid = (lanes <= lax.broadcasted_iota(jnp.int32, (64, T), 0)) | (lanes >= 64)
        rh, rl = split(jnp.where(valid, raw[0:64, :], 0.0))
        lower = jnp.where(lanes < 64, 0.0, block[64:])
        lower = lower - (dot_tn(rh, rh) + dot_tn(rh, rl) + dot_tn(rl, rh))[64:]
        eliminate(lower, 64, store_lower)
        bh, bl = vh[here, :], vl[here, :]
        for tile in tiles:
            a_ref[tile, here] = a_ref[tile, here] - dot3(vh[tile, :], vl[tile, :], bh, bl)
        nh, nl = vh[after, :], vl[after, :]
        next_block = a_ref[after, after] - dot3(nh, nl, nh, nl)
        at = lax.broadcasted_iota(jnp.int32, (T, T), 0)
        inverse = jnp.where(lax.broadcasted_iota(jnp.int32, (T, T), 1) <= at, raw[...], 0.0)
        li[...] = inverse
        lh, ll = split(inverse)
        ah, al = split(a_ref[after, here])
        h, l = split(dot3(ah, al, lh, ll))
        diag[...] = next_block - dot3(h, l, h, l)
        vh[after, here] = h
        vl[after, here] = l
        return 0

    lax.fori_loop(0, 4, block_column, 0)
    panel(3)


def schur(a_ref, vh, vl, item):
    for i, j in ((0, 0), (1, 0), (1, 1)):
        ri = slice(S + i * 256, S + i * 256 + 256)
        rj = slice(S + j * 256, S + j * 256 + 256)
        c = a_ref[ri, rj] - dot3(vh[ri, :], vl[ri, :], vh[rj, :], vl[rj, :])
        for p, (bi, bj) in enumerate(PAIRS):
            if bi // 2 == i and bj // 2 == j:
                ro, co = (bi % 2) * T, (bj % 2) * T
                item[2 * p] = c[ro : ro + 64, co : co + T]
                item[2 * p + 1] = c[ro + 64 : ro + T, co : co + T]


def schur_rhs(a_ref, vh, vl, rhs_t):
    rows = slice(FRONT, ROWS)
    for j in range(2):
        rj = slice(S + j * 256, S + j * 256 + 256)
        rhs_t[:, j * 256 : j * 256 + 256] = a_ref[rows, rj] - dot3(
            vh[rows, :], vl[rows, :], vh[rj, :], vl[rj, :]
        )


def partner_of(leaf, t):
    x, y = lax.rem(leaf, X_LEN), leaf // X_LEN
    one = jnp.int32(1)
    span_x = jnp.where(t == 0, 2 * one, jnp.where(t == 1, 4 * one, one))
    span_y = jnp.where(t == 2, 2 * one, jnp.where(t == 3, 4 * one, jnp.where(t == 4, 8 * one, one)))
    px = x - lax.rem(x, span_x) + span_x - 1 - lax.rem(x, span_x)
    py = y - lax.rem(y, span_y) + span_y - 1 - lax.rem(y, span_y)
    return py * X_LEN + px


def kernel(
    upd_ref, rhs_ref, map_ref, coef_ref,
    out_upd, out_rhs, out_sol,
    full, slab_out, slab_in, last_out, last_in,
    own, own_h, sib, sib_h, p_own, p_sib, ch, cl, th, tl, x0, x1, a_ref, li, raw, diag, vh, vl, y_t, y_kept,
    ring_send, ring_recv, core_send, core_recv, slab_send, slab_recv, last_send, last_recv,
    put_send, put_recv, row_send, row_recv, near_send, near_recv, far_send, far_recv,
    rhs_send, rhs_recv, loc,
):
    leaf = lax.axis_index("leaf")
    row = lax.axis_index("row")
    col = lax.axis_index("col")
    other = 1 - col
    beside = row + 1 - 2 * lax.rem(row, 2)
    quarter = 2 * lax.rem(row, 2) + col
    quarter_row = 2 * lax.rem(beside, 2) + col

    def to_peer(src, dst, send_sem, recv_sem, device):
        return pltpu.make_async_remote_copy(
            src_ref=src, dst_ref=dst, send_sem=send_sem, recv_sem=recv_sem,
            device_id=device, device_id_type=MESH,
        )

    barrier = pltpu.get_barrier_semaphore()
    peers = [lax.rem(row + d, Z_LEN) for d in range(Z_LEN)]
    targets = [(leaf, peers[d], col) for d in range(1, Z_LEN)] + [(leaf, row, other), (leaf, beside, other)]
    targets += [(partner_of(leaf, t), row, col) for t in range(LEVELS)]
    for target in targets:
        pl.semaphore_signal(barrier, inc=1, device_id=target, device_id_type=MESH)

    here = (pl.ds(pl.multiple_of(row * 64, 64), 64), pl.ds(pl.multiple_of(col * 256, 256), 256))
    put_own = pltpu.make_async_copy(upd_ref.at[0], full.at[here], loc)
    put_own.start()
    slabs = rhs_ref[0].T
    for r in range(Z_LEN):
        slab_out[r, :, 0:64] = slabs[r * 16 : r * 16 + 16, :]
    put_own.wait()
    pl.semaphore_wait(barrier, len(targets))

    up, down = peers[1], peers[Z_LEN - 1]

    def ring_copy(owner, to, way, step):
        rows = pl.ds(pl.multiple_of(owner * 64, 64), 64)
        ref = full.at[rows, here[1]]
        return to_peer(
            ref, ref, ring_send.at[way, step], ring_recv.at[way, step], (leaf, to, col)
        )

    def core_copy(owner, half, n):
        rows = pl.ds(pl.multiple_of(owner * 64, 64), 64)
        ref = full.at[rows, pl.ds(pl.multiple_of(half * 256, 256), 256)]
        return to_peer(ref, ref, core_send.at[n], core_recv.at[n], (leaf, row, other))

    sends = [ring_copy(row, up, 0, 0), ring_copy(row, down, 1, 0), core_copy(row, col, 0)]
    for copy in sends:
        copy.start()
    slab_copies = [
        to_peer(
            slab_out.at[peers[d]], slab_in.at[row], slab_send.at[d], slab_recv.at[d],
            (leaf, peers[d], col),
        )
        for d in range(1, Z_LEN)
    ]
    for copy in slab_copies:
        copy.start()
    slab_in[row] = slab_out[row]
    owners = [row]
    for step in range(4):
        for way, owner, to in ((0, peers[7 - step], up), (1, peers[1 + step], down)):
            if way == 1 and step == 3:
                continue
            ring_copy(owner, to, way, step).wait_recv()
            if step + 1 < 4 - way:
                sends.append(ring_copy(owner, to, way, step + 1))
                sends[-1].start()
            sends.append(core_copy(owner, col, len(owners)))
            sends[-1].start()
            owners.append(owner)
    for n, owner in enumerate(owners):
        core_copy(owner, other, n).wait_recv()
    for copy in sends:
        copy.wait_send()
    for copy in slab_copies:
        copy.wait()

    def puts(t):
        partner = partner_of(leaf, t)
        return [
            to_peer(
                own.at[t, 5 * quarter + q], sib.at[t, 5 * quarter + q],
                put_send.at[q], put_recv.at[t, q], (partner, row, col),
            )
            for q in range(5)
        ]

    def put_rhs(t):
        return to_peer(
            own_h.at[t], sib_h.at[t], rhs_send, rhs_recv.at[t], (partner_of(leaf, t), row, col)
        )

    for p, (i, j) in enumerate(PAIRS):
        for half in range(2):
            lo = i * T + half * 64
            own[0, 2 * p + half] = full[lo : lo + 64, j * T : j * T + T]
    for copy in puts(0):
        copy.start()
    for i in range(4):
        own_h[0, :, i * T : i * T + T] = jnp.concatenate(
            [slab_in[2 * i, :, 0:64], slab_in[2 * i + 1, :, 0:64]], axis=1
        )
    put_rhs(0).start()

    def level(t, _):
        bit = lax.rem(leaf >> t, 2)
        front = 32 - (32 >> t) + (leaf >> (t + 1))

        def share(part, q, send, recv, device):
            ref = sib.at[t, 5 * part + q]
            return to_peer(ref, ref, send.at[q], recv.at[t, q], device)

        over_core, over_row = (leaf, row, other), (leaf, beside, col)
        arrive = puts(t)
        to_near = [share(quarter, q, near_send, near_recv, over_core) for q in range(5)]
        to_row = [share(quarter, q, row_send, row_recv, over_row) for q in range(5)]
        to_far = [share(quarter_row, q, far_send, far_recv, over_core) for q in range(4)]
        to_far.append(share(quarter, 4, far_send, far_recv, (leaf, beside, other)))

        def pass_on(q):
            arrive[q].wait_recv()
            to_row[q].start()
            if q == 4:
                to_far[q].start()
            to_near[q].start()

        def pass_far(q):
            to_row[q].wait_recv()
            if q < 4:
                to_far[q].start()

        build_one_hot(map_ref[front, pl.ds(bit, 1), :], p_own)
        expand(own.at[t], ch, cl)
        spread_rows(0, p_own, ch, cl, th, tl)
        spread_cols(0, p_own, th, tl, x0)
        pass_on(0)
        spread_rows(1, p_own, ch, cl, th, tl)
        pass_on(1)
        spread_cols(1, p_own, th, tl, x0)
        pass_on(2)
        spread_rows(2, p_own, ch, cl, th, tl)
        pass_on(3)
        pass_far(0)
        spread_cols(2, p_own, th, tl, x0)
        pass_on(4)
        pass_far(1)
        spread_rows(3, p_own, ch, cl, th, tl)
        pass_far(2)
        spread_cols(3, p_own, th, tl, x0)
        pass_far(3)
        build_one_hot(map_ref[front, pl.ds(1 - bit, 1), :], p_sib)
        pass_far(4)
        spread_rhs(own_h.at[t], p_own, x0)
        clear(li, vh, vl)
        put_rhs(t).wait()
        spread_rhs(sib_h.at[t], p_sib, x1)
        for q in range(5):
            to_near[q].wait_recv()
            to_far[q].wait_recv()
        expand(sib.at[t], ch, cl)
        for i in range(4):
            spread_rows(i, p_sib, ch, cl, th, tl)
        for i in range(4):
            spread_cols(i, p_sib, th, tl, x1, first=0 if i < 2 else 2)
        for q in range(5):
            for copy in (arrive[q], to_near[q], to_row[q], to_far[q]):
                copy.wait_send()
        combine(x0, x1, coef_ref[pl.ds(front, 1), :], a_ref)
        factor(a_ref, x0, x1, p_sib, th, tl, li, raw, diag, vh, vl, y_t)

        @pl.when(t < LEVELS - 1)
        def _():
            schur(a_ref, vh, vl, own.at[t + 1])
            for copy in puts(t + 1):
                copy.start()
            schur_rhs(a_ref, vh, vl, own_h.at[t + 1])
            put_rhs(t + 1).start()

        low = lax.rem(leaf, 2 << t)
        keep = (low == (1 << t)) | ((t == LEVELS - 1) & (lax.rem(leaf, 1 << t) == 0))

        @pl.when(keep)
        def _():
            y_kept[...] = y_t[...]

        return 0

    lax.fori_loop(0, LEVELS, level, 0)

    schur_rhs(a_ref, vh, vl, own_h.at[LEVELS])
    for r in range(Z_LEN):
        last_out[r, 0:16, 0:64] = own_h[LEVELS, :, r * 64 : r * 64 + 64]
        last_out[r, 16:32, 0:64] = y_kept[:, r * 64 : r * 64 + 64]
    last_copies = [
        to_peer(
            last_out.at[peers[d]], last_in.at[row], last_send.at[d], last_recv.at[d],
            (leaf, peers[d], col),
        )
        for d in range(1, Z_LEN)
    ]
    for copy in last_copies:
        copy.start()
    last_in[row] = last_out[row]
    schur(a_ref, vh, vl, own.at[LEVELS])
    for p, (i, j) in enumerate(PAIRS):
        block = jnp.concatenate([own[LEVELS, 2 * p], own[LEVELS, 2 * p + 1]], axis=0)
        full[i * T : i * T + T, j * T : j * T + T] = block
        if i != j:
            full[j * T : j * T + T, i * T : i * T + T] = block.T
    out_upd[...] = full[here]
    for copy in last_copies:
        copy.wait()
    out_rhs[...] = jnp.concatenate([last_in[r, 0:16, 0:64] for r in range(Z_LEN)], axis=0).T
    out_sol[0] = jnp.concatenate([last_in[r, 16:32, 0:64] for r in range(Z_LEN)], axis=0).T


def per_device(leaf_update, leaf_rhs, child_rows, separator_coef):
    vmem = pl.BlockSpec(memory_space=pltpu.VMEM)
    dma = pltpu.SemaphoreType.DMA
    return pl.pallas_call(
        kernel,
        name="multifrontal",
        out_shape=(
            jax.ShapeDtypeStruct((64, 256), F32),
            jax.ShapeDtypeStruct((64, T), F32),
            jax.ShapeDtypeStruct((1, 64, T), F32),
        ),
        in_specs=[vmem] * 4,
        out_specs=(vmem,) * 3,
        scratch_shapes=[
            pltpu.VMEM((S, S), F32),
            pltpu.VMEM((Z_LEN, 16, T), F32),
            pltpu.VMEM((Z_LEN, 16, T), F32),
            pltpu.VMEM((Z_LEN, 32, T), F32),
            pltpu.VMEM((Z_LEN, 32, T), F32),
            pltpu.VMEM((LEVELS + 1, 20, 64, T), F32),
            pltpu.VMEM((LEVELS + 1, 16, S), F32),
            pltpu.VMEM((LEVELS, 20, 64, T), F32),
            pltpu.VMEM((LEVELS, 16, S), F32),
            pltpu.VMEM((FRONT, S), BF16),
            pltpu.VMEM((FRONT, S), BF16),
            pltpu.VMEM((S, S), BF16),
            pltpu.VMEM((S, S), BF16),
            pltpu.VMEM((FRONT, S), BF16),
            pltpu.VMEM((FRONT, S), BF16),
            pltpu.VMEM((ROWS, FRONT), F32),
            pltpu.VMEM((ROWS, FRONT), F32),
            pltpu.VMEM((ROWS, FRONT), F32),
            pltpu.VMEM((T, T), F32),
            pltpu.VMEM((T, T), F32),
            pltpu.VMEM((T, T), F32),
            pltpu.VMEM((ROWS, S), BF16),
            pltpu.VMEM((ROWS, S), BF16),
            pltpu.VMEM((16, S), F32),
            pltpu.VMEM((16, S), F32),
            dma((2, 4)), dma((2, 4)),
            dma((8,)), dma((8,)),
            dma((8,)), dma((8,)),
            dma((8,)), dma((8,)),
            dma((5,)), dma((LEVELS, 5)),
            dma((5,)), dma((LEVELS, 5)),
            dma((5,)), dma((LEVELS, 5)),
            dma((5,)), dma((LEVELS, 5)),
            dma, dma((LEVELS,)),
            dma,
        ],
        compiler_params=pltpu.CompilerParams(
            collective_id=0, has_side_effects=True, vmem_limit_bytes=56 * 1024 * 1024
        ),
    )(leaf_update, leaf_rhs, child_rows, separator_coef)


def solution(mesh):
    in_specs = (P("leaf", "row", "col"), P("leaf", "row", "col"), P(), P())
    out_specs = (P("row", "col"), P("row", "col"), P("leaf", "row", "col"))
    return jax.shard_map(
        per_device, mesh=mesh, in_specs=in_specs, out_specs=out_specs, check_vma=False
    )
```

```python
import functools

import jax
import jax.numpy as jnp
from jax import lax
from jax.experimental import pallas as pl
from jax.experimental.pallas import tpu as pltpu
from jax.sharding import PartitionSpec as P

F32 = jnp.float32
BF16 = jnp.bfloat16
MESH = pl.DeviceIdType.MESH
LEVELS = 5
X_LEN, Z_LEN = 4, 8
S = 512
T = 128
FRONT = 2 * S
ROWS = FRONT + 16
PAIRS = [(i, j) for i in range(4) for j in range(i + 1)]


def dot_nt(a, b):
    return lax.dot_general(a, b, (((1,), (1,)), ((), ())), preferred_element_type=F32)


def split(x):
    high = x.astype(BF16)
    return high, (x - high.astype(F32)).astype(BF16)


def dot_tn(a, b):
    return lax.dot_general(a, b, (((0,), (0,)), ((), ())), preferred_element_type=F32)


def dot3(ah, al, bh, bl):
    return dot_nt(ah, bh) + dot_nt(ah, bl) + dot_nt(al, bh)


def eliminate(a, base, store_row):
    m, n = a.shape
    lane = lax.broadcasted_iota(jnp.int32, (8, n), 1)
    sub = lax.broadcasted_iota(jnp.int32, (8, n), 0)

    def spread_col(rows, at):
        return jnp.broadcast_to(rows[:, at : at + 1], rows.shape)

    top = [spread_col(a[:8], base + j) for j in range(8)]
    for lo in range(0, m, 8):
        at = base + lo
        inside = (lane >= at) & (lane < at + 8)
        head = jnp.where(inside, jnp.where(lane - at == sub, 1.0, 0.0), a[:8])
        left = m - lo - 8
        if left:
            low = [spread_col(a[8:], at + j) for j in range(8)]
            ahead = [spread_col(a[8:16], at + 8 + j) for j in range(8)]
            a = jnp.concatenate(
                [jnp.where(inside, 0.0, a[i : i + 8]) for i in range(8, left + 8, 8)], axis=0
            )
        for k in range(8):
            pivot = top[k][k : k + 1]
            inverse = 1.0 / pivot
            row = head[k : k + 1]
            store_row(lo + k, row * lax.rsqrt(pivot))
            if left:
                below = low[k] * inverse
            for j in range(k + 1, 8):
                factor_row = top[k][j : j + 1]
                top[j] = top[j] - (top[k] * factor_row) * inverse
                if left:
                    low[j] = low[j] - below * factor_row
            if left:
                for j in range(8):
                    ahead[j] = ahead[j] - below[:8] * low[k][j : j + 1]
                a = a - below * row
            if k < 7:
                head = head - (top[k] * inverse) * row
        if left:
            top = ahead


def build_one_hot(map_row, p_ref):
    for lo in range(0, FRONT, 256):
        at = lax.broadcasted_iota(jnp.int32, (256, S), 0) + lo
        p_ref[lo : lo + 256, :] = jnp.where(at == map_row, 1.0, 0.0).astype(BF16)


def expand(item, ch, cl):
    for p, (i, j) in enumerate(PAIRS):
        block = jnp.concatenate([item[2 * p], item[2 * p + 1]], axis=0)
        h, l = split(block)
        ch[i * T : i * T + T, j * T : j * T + T] = h
        cl[i * T : i * T + T, j * T : j * T + T] = l
        if i != j:
            h, l = split(block.T)
            ch[j * T : j * T + T, i * T : i * T + T] = h
            cl[j * T : j * T + T, i * T : i * T + T] = l


def spread_rows(i, p_ref, ch, cl, th, tl):
    tile = slice(i * 256, i * 256 + 256)
    rows = p_ref[tile, :]
    th[tile, :] = dot_nt(rows, ch[...]).astype(BF16)
    tl[tile, :] = dot_nt(rows, cl[...]).astype(BF16)


def spread_cols(i, p_ref, th, tl, x_ref, first=0):
    tile = slice(i * 256, i * 256 + 256)
    for j in range(first, i + 1):
        cols = p_ref[j * 256 : j * 256 + 256, :]
        x_ref[tile, j * 256 : j * 256 + 256] = dot_nt(th[tile, :], cols) + dot_nt(tl[tile, :], cols)


def spread_rhs(rhs_t, p_ref, x_ref):
    both = jnp.concatenate(split(rhs_t[...]), axis=0)
    for j in range(4):
        x = dot_nt(both, p_ref[j * 256 : j * 256 + 256, :])
        x_ref[FRONT:ROWS, j * 256 : j * 256 + 256] = x[:16] + x[16:]


def combine(x0, x1, coef_row, a_ref):
    for i, j in ((0, 0), (1, 0), (1, 1)):
        at = (slice(i * 256, i * 256 + 256), slice(j * 256, j * 256 + 256))
        distance = (
            lax.broadcasted_iota(jnp.int32, (256, 256), 0)
            - lax.broadcasted_iota(jnp.int32, (256, 256), 1)
            + (i - j) * 256
        )
        diag = coef_row[:, j * 256 : j * 256 + 256] + 2.0
        stencil = jnp.where(distance == 0, diag, jnp.where(jnp.abs(distance) == 1, -1.0, 0.0))
        a_ref[at] = x0[at] + x1[at] + stencil
    for i, j in ((2, 2), (3, 2), (3, 3)):
        at = (slice(i * 256, i * 256 + 256), slice(j * 256, j * 256 + 256))
        a_ref[at] = x0[at] + x1[at]
    a_ref[FRONT:ROWS, :] = x0[FRONT:ROWS, :] + x1[FRONT:ROWS, :]


def clear(li, vh, vl):
    vh[...] = jnp.zeros_like(vh)
    vl[...] = jnp.zeros_like(vl)
    li[...] = jnp.zeros_like(li)


def factor(a_ref, x0, x1, p_sib, th, tl, li, raw, diag, vh, vl, y_t):
    diag[...] = a_ref[0:T, 0:T]
    tiles = [slice(0, 256), slice(256, 512), slice(512, 768), slice(768, ROWS)]

    def panel(k, tiles):
        here = pl.ds(pl.multiple_of(k * T, T), T)
        lh, ll = split(li[...])
        for tile in tiles:
            ah, al = split(a_ref[tile, here])
            v = dot3(ah, al, lh, ll)
            h, l = split(v)
            vh[tile, here] = h
            vl[tile, here] = l
            if tile.stop == ROWS:
                y_t[:, here] = v[256:]

    def block_column(k, _):
        here = pl.ds(pl.multiple_of(k * T, T), T)
        after = pl.ds(pl.multiple_of(k * T + T, T), T)
        block = diag[...]

        def store_upper(i, row):
            raw[i : i + 1, :] = row

        def store_lower(i, row):
            raw[64 + i : 65 + i, :] = row

        eliminate(block[:64], 0, store_upper)
        panel(jnp.maximum(k - 1, 0), tiles)
        for tile in (slice(512, 768), slice(768, FRONT)):
            x1[tile, here] = dot_nt(th[tile, :], p_sib[here, :]) + dot_nt(tl[tile, :], p_sib[here, :])
            a_ref[tile, here] = x0[tile, here] + x1[tile, here]
        lanes = lax.broadcasted_iota(jnp.int32, (64, T), 1)
        valid = (lanes <= lax.broadcasted_iota(jnp.int32, (64, T), 0)) | (lanes >= 64)
        rh, rl = split(jnp.where(valid, raw[0:64, :], 0.0))
        lower = jnp.where(lanes < 64, 0.0, block[64:])
        lower = lower - (dot_tn(rh, rh) + dot_tn(rh, rl) + dot_tn(rl, rh))[64:]
        eliminate(lower, 64, store_lower)
        bh, bl = vh[here, :], vl[here, :]
        for tile in tiles:
            a_ref[tile, here] = a_ref[tile, here] - dot3(vh[tile, :], vl[tile, :], bh, bl)
        nh, nl = vh[after, :], vl[after, :]
        next_block = a_ref[after, after] - dot3(nh, nl, nh, nl)
        at = lax.broadcasted_iota(jnp.int32, (T, T), 0)
        inverse = jnp.where(lax.broadcasted_iota(jnp.int32, (T, T), 1) <= at, raw[...], 0.0)
        li[...] = inverse
        lh, ll = split(inverse)
        ah, al = split(a_ref[after, here])
        h, l = split(dot3(ah, al, lh, ll))
        diag[...] = next_block - dot3(h, l, h, l)
        vh[after, here] = h
        vl[after, here] = l
        return 0

    lax.fori_loop(0, 4, block_column, 0)
    panel(3, tiles[2:])


def schur(a_ref, vh, vl, item):
    for i, j in ((0, 0), (1, 0), (1, 1)):
        ri = slice(S + i * 256, S + i * 256 + 256)
        rj = slice(S + j * 256, S + j * 256 + 256)
        c = a_ref[ri, rj] - dot3(vh[ri, :], vl[ri, :], vh[rj, :], vl[rj, :])
        for p, (bi, bj) in enumerate(PAIRS):
            if bi // 2 == i and bj // 2 == j:
                ro, co = (bi % 2) * T, (bj % 2) * T
                item[2 * p] = c[ro : ro + 64, co : co + T]
                item[2 * p + 1] = c[ro + 64 : ro + T, co : co + T]


def schur_rhs(a_ref, vh, vl, rhs_t):
    rows = slice(FRONT, ROWS)
    for j in range(2):
        rj = slice(S + j * 256, S + j * 256 + 256)
        rhs_t[:, j * 256 : j * 256 + 256] = a_ref[rows, rj] - dot3(
            vh[rows, :], vl[rows, :], vh[rj, :], vl[rj, :]
        )


def partner_of(leaf, t):
    x, y = lax.rem(leaf, X_LEN), leaf // X_LEN
    one = jnp.int32(1)
    span_x = jnp.where(t == 0, 2 * one, jnp.where(t == 1, 4 * one, one))
    span_y = jnp.where(t == 2, 2 * one, jnp.where(t == 3, 4 * one, jnp.where(t == 4, 8 * one, one)))
    px = x - lax.rem(x, span_x) + span_x - 1 - lax.rem(x, span_x)
    py = y - lax.rem(y, span_y) + span_y - 1 - lax.rem(y, span_y)
    return py * X_LEN + px


def kernel(
    upd_ref, rhs_ref, map_ref, coef_ref,
    out_upd, out_rhs, out_sol,
    full, slab_out, slab_in, last_out, last_in,
    own, own_h, sib, sib_h, p_own, p_sib, ch, cl, th, tl, x0, x1, a_ref, li, raw, diag, vh, vl, y_t, y_kept,
    ring_send, ring_recv, core_send, core_recv, slab_send, slab_recv, last_send, last_recv,
    put_send, put_recv, row_send, row_recv, near_send, near_recv, far_send, far_recv,
    rhs_send, rhs_recv, loc,
):
    leaf = lax.axis_index("leaf")
    row = lax.axis_index("row")
    col = lax.axis_index("col")
    other = 1 - col
    beside = row + 1 - 2 * lax.rem(row, 2)
    quarter = 2 * lax.rem(row, 2) + col
    quarter_row = 2 * lax.rem(beside, 2) + col

    def to_peer(src, dst, send_sem, recv_sem, device):
        return pltpu.make_async_remote_copy(
            src_ref=src, dst_ref=dst, send_sem=send_sem, recv_sem=recv_sem,
            device_id=device, device_id_type=MESH,
        )

    barrier = pltpu.get_barrier_semaphore()
    peers = [lax.rem(row + d, Z_LEN) for d in range(Z_LEN)]
    targets = [(leaf, peers[d], col) for d in range(1, Z_LEN)] + [(leaf, row, other), (leaf, beside, other)]
    targets += [(partner_of(leaf, t), row, col) for t in range(LEVELS)]
    for target in targets:
        pl.semaphore_signal(barrier, inc=1, device_id=target, device_id_type=MESH)

    here = (pl.ds(pl.multiple_of(row * 64, 64), 64), pl.ds(pl.multiple_of(col * 256, 256), 256))
    put_own = pltpu.make_async_copy(upd_ref.at[0], full.at[here], loc)
    put_own.start()
    slabs = rhs_ref[0].T
    for r in range(Z_LEN):
        slab_out[r, :, 0:64] = slabs[r * 16 : r * 16 + 16, :]
    put_own.wait()
    pl.semaphore_wait(barrier, len(targets))

    up, down = peers[1], peers[Z_LEN - 1]

    def ring_copy(owner, to, way, step, half):
        rows = pl.ds(pl.multiple_of(owner * 64, 64), 64)
        ref = full.at[rows, pl.ds(pl.multiple_of(col * 256 + half * T, T), T)]
        return to_peer(
            ref, ref, ring_send.at[way, step, half], ring_recv.at[way, step, half], (leaf, to, col)
        )

    def core_copy(owner, half, n):
        rows = pl.ds(pl.multiple_of(owner * 64, 64), 64)
        ref = full.at[rows, pl.ds(pl.multiple_of(half * 256, 256), 256)]
        return to_peer(ref, ref, core_send.at[n], core_recv.at[n], (leaf, row, other))

    sends = []
    for half in range(2):
        sends += [ring_copy(row, up, 0, 0, half), ring_copy(row, down, 1, 0, half)]
    sends.append(core_copy(row, col, 0))
    for copy in sends:
        copy.start()
    slab_copies = [
        to_peer(
            slab_out.at[peers[d]], slab_in.at[row], slab_send.at[d], slab_recv.at[d],
            (leaf, peers[d], col),
        )
        for d in range(1, Z_LEN)
    ]
    for copy in slab_copies:
        copy.start()
    slab_in[row] = slab_out[row]
    owners = [row]
    for step in range(4):
        ways = ((0, peers[7 - step], up), (1, peers[1 + step], down))[: 2 if step < 3 else 1]
        for half in range(2):
            for way, owner, to in ways:
                ring_copy(owner, to, way, step, half).wait_recv()
                if step + 1 < 4 - way:
                    sends.append(ring_copy(owner, to, way, step + 1, half))
                    sends[-1].start()
        for way, owner, to in ways:
            sends.append(core_copy(owner, col, len(owners)))
            sends[-1].start()
            owners.append(owner)
    for n, owner in enumerate(owners):
        core_copy(owner, other, n).wait_recv()
    for copy in sends:
        copy.wait_send()
    for copy in slab_copies:
        copy.wait()

    def puts(t):
        partner = partner_of(leaf, t)
        return [
            to_peer(
                own.at[t, 5 * quarter + q], sib.at[t, 5 * quarter + q],
                put_send.at[q], put_recv.at[t, q], (partner, row, col),
            )
            for q in range(5)
        ]

    def put_rhs(t):
        return to_peer(
            own_h.at[t], sib_h.at[t], rhs_send, rhs_recv.at[t], (partner_of(leaf, t), row, col)
        )

    for p, (i, j) in enumerate(PAIRS):
        for half in range(2):
            lo = i * T + half * 64
            own[0, 2 * p + half] = full[lo : lo + 64, j * T : j * T + T]
    for copy in puts(0):
        copy.start()
    for i in range(4):
        own_h[0, :, i * T : i * T + T] = jnp.concatenate(
            [slab_in[2 * i, :, 0:64], slab_in[2 * i + 1, :, 0:64]], axis=1
        )
    put_rhs(0).start()

    def level(t, _):
        bit = lax.rem(leaf >> t, 2)
        front = 32 - (32 >> t) + (leaf >> (t + 1))

        def share(part, q, send, recv, device):
            ref = sib.at[t, 5 * part + q]
            return to_peer(ref, ref, send.at[q], recv.at[t, q], device)

        over_core, over_row = (leaf, row, other), (leaf, beside, col)
        arrive = puts(t)
        to_near = [share(quarter, q, near_send, near_recv, over_core) for q in range(5)]
        to_row = [share(quarter, q, row_send, row_recv, over_row) for q in range(5)]
        to_far = [share(quarter_row, q, far_send, far_recv, over_core) for q in range(4)]
        to_far.append(share(quarter, 4, far_send, far_recv, (leaf, beside, other)))

        def pass_on(q):
            arrive[q].wait_recv()
            to_row[q].start()
            if q == 4:
                to_far[q].start()
            to_near[q].start()

        def pass_far(q):
            to_row[q].wait_recv()
            if q < 4:
                to_far[q].start()

        build_one_hot(map_ref[front, pl.ds(bit, 1), :], p_own)
        expand(own.at[t], ch, cl)
        spread_rows(0, p_own, ch, cl, th, tl)
        spread_cols(0, p_own, th, tl, x0)
        pass_on(0)
        spread_rows(1, p_own, ch, cl, th, tl)
        pass_on(1)
        spread_cols(1, p_own, th, tl, x0)
        pass_on(2)
        spread_rows(2, p_own, ch, cl, th, tl)
        pass_on(3)
        pass_far(0)
        spread_cols(2, p_own, th, tl, x0)
        pass_on(4)
        pass_far(1)
        spread_rows(3, p_own, ch, cl, th, tl)
        pass_far(2)
        spread_cols(3, p_own, th, tl, x0)
        pass_far(3)
        build_one_hot(map_ref[front, pl.ds(1 - bit, 1), :], p_sib)
        pass_far(4)
        spread_rhs(own_h.at[t], p_own, x0)
        clear(li, vh, vl)
        put_rhs(t).wait()
        spread_rhs(sib_h.at[t], p_sib, x1)
        for q in range(5):
            to_near[q].wait_recv()
            to_far[q].wait_recv()
        expand(sib.at[t], ch, cl)
        for i in range(4):
            spread_rows(i, p_sib, ch, cl, th, tl)
        for i in range(4):
            spread_cols(i, p_sib, th, tl, x1, first=0 if i < 2 else 2)
        for q in range(5):
            for copy in (arrive[q], to_near[q], to_row[q], to_far[q]):
                copy.wait_send()
        combine(x0, x1, coef_ref[pl.ds(front, 1), :], a_ref)
        factor(a_ref, x0, x1, p_sib, th, tl, li, raw, diag, vh, vl, y_t)

        @pl.when(t < LEVELS - 1)
        def _():
            schur(a_ref, vh, vl, own.at[t + 1])
            for copy in puts(t + 1):
                copy.start()
            schur_rhs(a_ref, vh, vl, own_h.at[t + 1])
            put_rhs(t + 1).start()

        low = lax.rem(leaf, 2 << t)
        keep = (low == (1 << t)) | ((t == LEVELS - 1) & (lax.rem(leaf, 1 << t) == 0))

        @pl.when(keep)
        def _():
            y_kept[...] = y_t[...]

        return 0

    lax.fori_loop(0, LEVELS, level, 0)

    schur_rhs(a_ref, vh, vl, own_h.at[LEVELS])
    for r in range(Z_LEN):
        last_out[r, 0:16, 0:64] = own_h[LEVELS, :, r * 64 : r * 64 + 64]
        last_out[r, 16:32, 0:64] = y_kept[:, r * 64 : r * 64 + 64]
    last_copies = [
        to_peer(
            last_out.at[peers[d]], last_in.at[row], last_send.at[d], last_recv.at[d],
            (leaf, peers[d], col),
        )
        for d in range(1, Z_LEN)
    ]
    for copy in last_copies:
        copy.start()
    last_in[row] = last_out[row]
    schur(a_ref, vh, vl, own.at[LEVELS])
    for p, (i, j) in enumerate(PAIRS):
        block = jnp.concatenate([own[LEVELS, 2 * p], own[LEVELS, 2 * p + 1]], axis=0)
        full[i * T : i * T + T, j * T : j * T + T] = block
        if i != j:
            full[j * T : j * T + T, i * T : i * T + T] = block.T
    out_upd[...] = full[here]
    for copy in last_copies:
        copy.wait()
    out_rhs[...] = jnp.concatenate([last_in[r, 0:16, 0:64] for r in range(Z_LEN)], axis=0).T
    out_sol[0] = jnp.concatenate([last_in[r, 16:32, 0:64] for r in range(Z_LEN)], axis=0).T


def per_device(leaf_update, leaf_rhs, child_rows, separator_coef):
    vmem = pl.BlockSpec(memory_space=pltpu.VMEM)
    dma = pltpu.SemaphoreType.DMA
    return pl.pallas_call(
        kernel,
        name="multifrontal",
        out_shape=(
            jax.ShapeDtypeStruct((64, 256), F32),
            jax.ShapeDtypeStruct((64, T), F32),
            jax.ShapeDtypeStruct((1, 64, T), F32),
        ),
        in_specs=[vmem] * 4,
        out_specs=(vmem,) * 3,
        scratch_shapes=[
            pltpu.VMEM((S, S), F32),
            pltpu.VMEM((Z_LEN, 16, T), F32),
            pltpu.VMEM((Z_LEN, 16, T), F32),
            pltpu.VMEM((Z_LEN, 32, T), F32),
            pltpu.VMEM((Z_LEN, 32, T), F32),
            pltpu.VMEM((LEVELS + 1, 20, 64, T), F32),
            pltpu.VMEM((LEVELS + 1, 16, S), F32),
            pltpu.VMEM((LEVELS, 20, 64, T), F32),
            pltpu.VMEM((LEVELS, 16, S), F32),
            pltpu.VMEM((FRONT, S), BF16),
            pltpu.VMEM((FRONT, S), BF16),
            pltpu.VMEM((S, S), BF16),
            pltpu.VMEM((S, S), BF16),
            pltpu.VMEM((FRONT, S), BF16),
            pltpu.VMEM((FRONT, S), BF16),
            pltpu.VMEM((ROWS, FRONT), F32),
            pltpu.VMEM((ROWS, FRONT), F32),
            pltpu.VMEM((ROWS, FRONT), F32),
            pltpu.VMEM((T, T), F32),
            pltpu.VMEM((T, T), F32),
            pltpu.VMEM((T, T), F32),
            pltpu.VMEM((ROWS, S), BF16),
            pltpu.VMEM((ROWS, S), BF16),
            pltpu.VMEM((16, S), F32),
            pltpu.VMEM((16, S), F32),
            dma((2, 4, 2)), dma((2, 4, 2)),
            dma((8,)), dma((8,)),
            dma((8,)), dma((8,)),
            dma((8,)), dma((8,)),
            dma((5,)), dma((LEVELS, 5)),
            dma((5,)), dma((LEVELS, 5)),
            dma((5,)), dma((LEVELS, 5)),
            dma((5,)), dma((LEVELS, 5)),
            dma, dma((LEVELS,)),
            dma,
        ],
        compiler_params=pltpu.CompilerParams(
            collective_id=0, has_side_effects=True, vmem_limit_bytes=56 * 1024 * 1024
        ),
    )(leaf_update, leaf_rhs, child_rows, separator_coef)


def solution(mesh):
    in_specs = (P("leaf", "row", "col"), P("leaf", "row", "col"), P(), P())
    out_specs = (P("row", "col"), P("row", "col"), P("leaf", "row", "col"))
    return jax.shard_map(
        per_device, mesh=mesh, in_specs=in_specs, out_specs=out_specs, check_vma=False
    )
```
